128 devices in a mesh: blk: 16 (over z_hi, y, core), row: 8 (over x, z_lo).
Axes of the slice: x: 4, y: 4, z: 4 (z_hi: 2, z_lo: 2; z = z_hi * 2 + z_lo), core: 2. Of those that a mesh axis runs over, the one named last changes fastest.
Arguments:
- points: bfloat16 [262144, 128], P(('blk', 'row')), may hold values from -42 to 42
- feature_scale: float32 [128], replicated, may hold values from 0.7 to 1.6
- directions: float32 [262144, 32], P(('blk', 'row')), may hold values from -6 to 6
- accumulated: float32 [262144, 32], P(('blk', 'row')), may hold values from -2 to 2
- plan: int32 [2, 16], replicated, may hold values from 0 to 15, as said below
Outputs:
- product: float32 [262144, 32], P(('blk', 'row'))
- curvature: float32 [32], replicated
The draws below stay inside these ranges and needn't reach their ends.
Inputs may be any that keep to these rules, and one draw needn't show every extreme that they name: `plan`: row k gives every block's partner in round k: block i meets block i XOR m_k, with one mask m_k of 1 to 15 for the whole row; the masks of the 2 rows differ.
All inputs are finite; a program needn't handle non-finite values.
Results may differ from the reference program's by a relative error of at most 0.0075.
Values may be sent and summed in bfloat16 or wider, within the bound.
A program may use at most 128 MiB of HBM per device.

```python
import math
import jax
import jax.numpy as jnp
from jax import lax

F = 128
R = 32
ROUNDS = 2
NBLK = 16
BLK = 16384
NPTS = 262144


def draw_plan(key, part):
    key = jax.random.fold_in(key, 11)
    masks = jax.random.permutation(key, NBLK - 1)[:ROUNDS].astype(jnp.int32) + 1
    blocks = jnp.arange(NBLK, dtype=jnp.int32)
    return jnp.bitwise_xor(blocks[None, :], masks[:, None]).astype(jnp.int32)


def draw_points(key, part):
    key = jax.random.fold_in(key, 5)
    pick_key, value_key = jax.random.split(key, 2)
    order = jax.random.permutation(pick_key, F)
    chosen = order < 8
    widths = jnp.where(chosen, 0.625 * math.sqrt(F), 2.0).astype(jnp.float32)
    base = jnp.clip(jax.random.normal(value_key, (NPTS, F), jnp.float32), -6.0, 6.0)
    limit = float(F // 3)
    values = jnp.clip(base * widths[None, :], -limit, limit)
    return values.astype(jnp.bfloat16)


def block_scale(stream_key, shape, cuts, least, high):
    factor_of, own = 1.0, jax.random.fold_in(stream_key, 6)
    for position, parts in cuts:
        steps = jnp.exp(jax.random.uniform(jax.random.fold_in(own, position), (parts,), jnp.float32, least / len(cuts), high / len(cuts)))
        factor_of = factor_of * jnp.repeat(steps, shape[position] // parts).reshape([-1 if axis == position else 1 for axis in range(len(shape))])
    return factor_of


def gaussian(stream_key, shape, deviation, most, cuts=(), kind=jnp.bfloat16):
    entries = deviation * jax.random.normal(stream_key, shape, jnp.float32)
    if cuts:
        entries = entries * block_scale(stream_key, shape, cuts, -0.22, 0.18)
    return jnp.clip(entries, -most, most).astype(kind)


def setup_inputs(seed: int = 0) -> dict:
    key_of = jax.random.split(jax.random.key(seed), 6)
    return {
        "points": draw_points(jax.random.fold_in(key_of[5], 71), 0),
        "feature_scale": jnp.clip(jnp.exp(jax.random.uniform(key_of[1], (F,), jnp.float32, math.log(0.7), math.log(1.6))), 0.7, 1.6),
        "directions": gaussian(key_of[2], (NPTS, R), 1.0, 6.0, ((0, 128),), jnp.float32),
        "accumulated": gaussian(key_of[3], (NPTS, R), 0.25, 2.0, ((0, 128),), jnp.float32),
        "plan": draw_plan(jax.random.fold_in(key_of[5], 71), 0),
    }


def kernel_pass(row_z, col_z, col_p):
    amplitude = 512.0 / math.sqrt(BLK)
    cols_wide = min(BLK, 2048)
    num_blocks = BLK // cols_wide
    row_sq = lax.optimization_barrier(jnp.sum(jnp.square(row_z.astype(jnp.float32)), axis=1))
    blocks_z = col_z.reshape(num_blocks, cols_wide, col_z.shape[1])
    blocks_p = col_p.reshape(num_blocks, cols_wide, col_p.shape[1])

    def column_step(own_part, pieces):
        piece_z, piece_p = pieces
        col_sq = lax.optimization_barrier(jnp.sum(jnp.square(piece_z.astype(jnp.float32)), axis=1))
        inner_prod = lax.dot_general(row_z, piece_z, (((1,), (1,)), ((), ())), preferred_element_type=jnp.float32)
        kernel = (amplitude * jnp.exp(-0.5 * (row_sq[:, None] + col_sq[None, :] - 2.0 * inner_prod))).astype(jnp.bfloat16)
        return (own_part + jnp.dot(kernel, piece_p, preferred_element_type=jnp.float32), None)
    start_val = jnp.zeros((row_z.shape[0], col_p.shape[1]), jnp.float32)
    own_part, unused = lax.scan(column_step, start_val, (blocks_z, blocks_p))
    return own_part

def reference(points, feature_scale, directions, accumulated, plan):
    scaled = (points.astype(jnp.float32) * feature_scale[None, :] / math.sqrt(F)).astype(jnp.bfloat16)
    dirs = directions.astype(jnp.bfloat16)

    def one_block(block_idx):
        row_start = (block_idx * BLK).astype(jnp.int32)
        row_z = lax.dynamic_slice_in_dim(scaled, row_start, BLK, 0)
        summed = lax.dynamic_slice_in_dim(accumulated, row_start, BLK, 0)
        for round_idx in range(ROUNDS):
            partner = plan[round_idx, block_idx].astype(jnp.int32)
            col_start = (partner * BLK).astype(jnp.int32)
            col_z = lax.dynamic_slice_in_dim(scaled, col_start, BLK, 0)
            col_p = lax.dynamic_slice_in_dim(dirs, col_start, BLK, 0)
            summed = summed + kernel_pass(row_z, col_z, col_p)
        return summed
    product = lax.map(one_block, jnp.arange(NBLK, dtype=jnp.int32)).reshape(NPTS, R)
    curvature = lax.optimization_barrier(jnp.sum(dirs.astype(jnp.float32) * product, axis=0)) / NPTS
    return (product, curvature)
```

```python
import functools
import math

import jax
import jax.numpy as jnp
from jax import lax
from jax.experimental import pallas as pl
from jax.experimental.pallas import tpu as pltpu
from jax.sharding import PartitionSpec as P

F32 = jnp.float32
BF16 = jnp.bfloat16
CHUNK = 256
UNROLL = 8


def widen(z, mine):
    n = -0.5 * jnp.sum(jnp.square(z.astype(F32)), axis=1, keepdims=True)
    high = n.astype(BF16).astype(F32)
    mid = (n - high).astype(BF16).astype(F32)
    low = n - high - mid
    lane = lax.broadcasted_iota(jnp.int32, z.shape, 1)
    own, other = (0, 3) if mine else (3, 0)
    one = jnp.where((lane >= other) & (lane < other + 3), 1.0, 0.0)
    pieces = jnp.where(
        lane == own, high, jnp.where(lane == own + 1, mid, jnp.where(lane == own + 2, low, one))
    )
    return pieces.astype(BF16)


def tile_kernel(rows, a0, a1, b, fwd, back, wide_a, wide_b, dirs_a, k0, k1, t0, t1):
    feat = a0.shape[1]
    group = rows // feat
    for half, src in enumerate((a0, a1)):
        for piece in range(rows // 512):
            part = src[pl.ds(piece * 512, 512), :]
            at = pl.ds(half * rows + piece * 512, 512)
            wide_a[at, :feat] = part
            wide_a[at, feat:] = widen(part, True)
        for g in range(group):
            dirs_a[:, pl.ds(half * rows + g * feat, feat)] = src[pl.ds(rows + g * 32, 32), :]
    for piece in range(rows // 512):
        part = b[pl.ds(piece * 512, 512), :]
        at = pl.ds(piece * 512, 512)
        wide_b[at, :feat] = part
        wide_b[at, feat:] = widen(part, False)
    fwd[...] = jnp.zeros_like(fwd)
    back[...] = jnp.zeros_like(back)
    steps = 2 * (rows // CHUNK)
    kernels = ((k0, t0), (k1, t1))

    def place(t):
        return pl.multiple_of((t % 2) * rows, rows), pl.multiple_of((t // 2) * CHUNK, CHUNK)

    def produce(t, slot):
        i, j = place(t)
        exponent = lax.dot_general(
            wide_a[pl.ds(i, rows), :],
            wide_b[pl.ds(j, CHUNK), :],
            (((1,), (1,)), ((), ())),
            preferred_element_type=F32,
        )
        kernel = jnp.exp(exponent).astype(BF16)
        kernels[slot][0][...] = kernel
        kernels[slot][1][...] = kernel.T

    def consume(t, slot):
        i, j = place(t)
        at = pl.multiple_of(rows + (j // feat) * 32, 32)
        dirs_b = jnp.concatenate(
            [b[pl.ds(at + 32 * g, 32), :] for g in range(CHUNK // feat)], axis=1
        )
        fwd[:, pl.ds(i, rows)] += jnp.dot(
            dirs_b, kernels[slot][1][...], preferred_element_type=F32
        )
        back[:, pl.ds(j, CHUNK)] += jnp.dot(
            dirs_a[:, pl.ds(i, rows)], kernels[slot][0][...], preferred_element_type=F32
        )

    produce(0, 0)

    @pl.loop(0, steps // UNROLL)
    def _(h):
        for u in range(UNROLL):
            t = h * UNROLL + u
            produce(jnp.minimum(t + 1, steps - 1), (u + 1) % 2)
            consume(t, u % 2)


def tile_pass(a0, a1, b, rows):
    feat = a0.shape[1]
    return pl.pallas_call(
        functools.partial(tile_kernel, rows),
        out_shape=(
            jax.ShapeDtypeStruct((32, 2 * rows), F32),
            jax.ShapeDtypeStruct((32, rows), F32),
        ),
        in_specs=[pl.BlockSpec(memory_space=pltpu.VMEM)] * 3,
        out_specs=[pl.BlockSpec(memory_space=pltpu.VMEM)] * 2,
        scratch_shapes=[
            pltpu.VMEM((2 * rows, 2 * feat), BF16),
            pltpu.VMEM((rows, 2 * feat), BF16),
            pltpu.VMEM((32, 2 * rows), BF16),
            pltpu.VMEM((rows, CHUNK), BF16),
            pltpu.VMEM((rows, CHUNK), BF16),
            pltpu.VMEM((CHUNK, rows), BF16),
            pltpu.VMEM((CHUNK, rows), BF16),
        ],
        compiler_params=pltpu.CompilerParams(vmem_limit_bytes=40 * 2**20),
        cost_estimate=pl.CostEstimate(
            flops=2 * 2 * rows * rows * 640, bytes_accessed=4 * 2**20, transcendentals=0
        ),
        name="tile_pass",
    )(a0, a1, b)


def mask_pairs(mask, blocks, rows, returning):
    pairs = []
    for blk in range(blocks):
        for row in range(rows):
            partner = blk ^ mask
            source_row = row ^ 6 if blk > partner else row
            here, there = blk * rows + row, partner * rows + source_row
            pairs.append((here, there) if returning else (there, here))
    return pairs


def route(payload, mask, returning):
    blocks, rows = lax.axis_size("blk"), lax.axis_size("row")
    branches = [
        functools.partial(
            lambda pairs, v: lax.ppermute(v, ("blk", "row"), pairs),
            mask_pairs(m, blocks, rows, returning),
        )
        for m in range(1, blocks)
    ]
    return lax.switch(mask - 1, branches, payload)


def row_swap(payload, flip):
    rows = lax.axis_size("row")
    return lax.ppermute(payload, "row", [(i, i ^ flip) for i in range(rows)])


def shards(points, feature_scale, directions, accumulated, plan):
    rows, feat = points.shape
    block_size = rows * lax.axis_size("row")
    total_points = block_size * lax.axis_size("blk")
    amplitude = 512.0 / math.sqrt(block_size)
    scaled = (points.astype(F32) * feature_scale[None, :] / math.sqrt(feat)).astype(BF16)
    dirs = directions.astype(BF16)
    packed = dirs.T.reshape(32, rows // feat, feat).transpose(1, 0, 2).reshape(-1, feat)
    payload = jnp.concatenate([scaled, packed], axis=0)
    masks = [plan[k, 0] for k in range(plan.shape[0])]
    beside = row_swap(payload, 1)
    near = [route(payload, m, False) for m in masks]
    far = [row_swap(v, 2) for v in near]
    fwd_near = [tile_pass(payload, beside, v, rows) for v in near]
    fwd_far = [tile_pass(payload, beside, v, rows) for v in far]
    fwd = fwd_near[0][0] + fwd_near[1][0] + fwd_far[0][0] + fwd_far[1][0]
    own, other = fwd[:, :rows], fwd[:, rows:]
    wide = dirs.astype(F32)
    dirs_beside = beside[rows:].reshape(rows // feat, 32, feat).transpose(1, 0, 2).reshape(32, rows)
    summed = (
        own
        + row_swap(other.astype(BF16), 1).astype(F32)
    )
    for k, m in enumerate(masks):
        returned = fwd_near[k][1] + row_swap(fwd_far[k][1].astype(BF16), 2).astype(F32)
        summed = summed + route(returned.astype(BF16), m, True).astype(F32)
    product = accumulated + amplitude * summed.T
    early = jnp.sum(wide * accumulated, axis=0) + (2.0 * amplitude) * (
        jnp.sum(wide.T * own, axis=1) + jnp.sum(dirs_beside.astype(F32) * other, axis=1)
    )
    curvature = lax.psum(early, ("blk", "row"))
    return (product, curvature / total_points)


def solution(mesh):
    return jax.shard_map(
        shards,
        mesh=mesh,
        in_specs=(
            P(("blk", "row"), None),
            P(),
            P(("blk", "row"), None),
            P(("blk", "row"), None),
            P(),
        ),
        out_specs=(P(("blk", "row"), None), P()),
        check_vma=False,
    )
```

```python
import functools
import math

import jax
import jax.numpy as jnp
from jax import lax
from jax.experimental import pallas as pl
from jax.experimental.pallas import tpu as pltpu
from jax.sharding import PartitionSpec as P

F32 = jnp.float32
BF16 = jnp.bfloat16
CHUNK = 256
UNROLL = 8


def widen(z, mine):
    n = -0.5 * jnp.sum(jnp.square(z.astype(F32)), axis=1, keepdims=True)
    high = n.astype(BF16).astype(F32)
    mid = (n - high).astype(BF16).astype(F32)
    low = n - high - mid
    lane = lax.broadcasted_iota(jnp.int32, z.shape, 1)
    own, other = (0, 3) if mine else (3, 0)
    one = jnp.where((lane >= other) & (lane < other + 3), 1.0, 0.0)
    pieces = jnp.where(
        lane == own, high, jnp.where(lane == own + 1, mid, jnp.where(lane == own + 2, low, one))
    )
    return pieces.astype(BF16)


def tile_kernel(rows, a0, a1, b, fwd, back, wide_a, wide_b, dirs_a, k0, k1, t0, t1):
    feat = a0.shape[1]
    group = rows // feat
    for half, src in enumerate((a0, a1)):
        for piece in range(rows // 512):
            part = src[pl.ds(piece * 512, 512), :]
            at = pl.ds(half * rows + piece * 512, 512)
            wide_a[at, :feat] = part
            wide_a[at, feat:] = widen(part, True)
        for g in range(group):
            dirs_a[:, pl.ds(half * rows + g * feat, feat)] = src[pl.ds(rows + g * 32, 32), :]
    for piece in range(rows // 512):
        part = b[pl.ds(piece * 512, 512), :]
        at = pl.ds(piece * 512, 512)
        wide_b[at, :feat] = part
        wide_b[at, feat:] = widen(part, False)
    fwd[...] = jnp.zeros_like(fwd)
    back[...] = jnp.zeros_like(back)
    steps = 2 * (rows // CHUNK)
    kernels = ((k0, t0), (k1, t1))

    def place(t):
        return pl.multiple_of((t % 2) * rows, rows), pl.multiple_of((t // 2) * CHUNK, CHUNK)

    def produce(t, slot):
        i, j = place(t)
        exponent = lax.dot_general(
            wide_a[pl.ds(i, rows), :],
            wide_b[pl.ds(j, CHUNK), :],
            (((1,), (1,)), ((), ())),
            preferred_element_type=F32,
        )
        kernel = jnp.exp(exponent).astype(BF16)
        kernels[slot][0][...] = kernel
        kernels[slot][1][...] = kernel.T

    def consume(t, slot):
        i, j = place(t)
        at = pl.multiple_of(rows + (j // feat) * 32, 32)
        dirs_b = jnp.concatenate(
            [b[pl.ds(at + 32 * g, 32), :] for g in range(CHUNK // feat)], axis=1
        )
        fwd[:, pl.ds(i, rows)] += jnp.dot(
            dirs_b, kernels[slot][1][...], preferred_element_type=F32
        )
        back[:, pl.ds(j, CHUNK)] += jnp.dot(
            dirs_a[:, pl.ds(i, rows)], kernels[slot][0][...], preferred_element_type=F32
        )

    produce(0, 0)

    @pl.loop(0, steps // UNROLL)
    def _(h):
        for u in range(UNROLL):
            t = h * UNROLL + u
            produce(jnp.minimum(t + 1, steps - 1), (u + 1) % 2)
            consume(t, u % 2)


def tile_pass(a0, a1, b, rows):
    feat = a0.shape[1]
    return pl.pallas_call(
        functools.partial(tile_kernel, rows),
        out_shape=(
            jax.ShapeDtypeStruct((32, 2 * rows), F32),
            jax.ShapeDtypeStruct((32, rows), F32),
        ),
        in_specs=[pl.BlockSpec(memory_space=pltpu.VMEM)] * 3,
        out_specs=[pl.BlockSpec(memory_space=pltpu.VMEM)] * 2,
        scratch_shapes=[
            pltpu.VMEM((2 * rows, 2 * feat), BF16),
            pltpu.VMEM((rows, 2 * feat), BF16),
            pltpu.VMEM((32, 2 * rows), BF16),
            pltpu.VMEM((rows, CHUNK), BF16),
            pltpu.VMEM((rows, CHUNK), BF16),
            pltpu.VMEM((CHUNK, rows), BF16),
            pltpu.VMEM((CHUNK, rows), BF16),
        ],
        compiler_params=pltpu.CompilerParams(vmem_limit_bytes=40 * 2**20),
        cost_estimate=pl.CostEstimate(
            flops=2 * 2 * rows * rows * 640, bytes_accessed=4 * 2**20, transcendentals=0
        ),
        name="tile_pass",
    )(a0, a1, b)


def sum_kernel(blocks, rows, x_ref, out_ref, by_row, by_blk, half, row_send, row_recv, blk_send, blk_recv):
    my_blk, my_row = lax.axis_index("blk"), lax.axis_index("row")
    row_peers = [(my_blk, lax.rem(my_row + k, rows)) for k in range(1, rows)]
    blk_peers = [(lax.rem(my_blk + k, blocks), my_row) for k in range(1, blocks)]
    barrier = pltpu.get_barrier_semaphore()
    for peer in row_peers + blk_peers:
        pl.semaphore_signal(barrier, inc=1, device_id=peer, device_id_type=pl.DeviceIdType.MESH)
    pl.semaphore_wait(barrier, rows + blocks - 2)

    def exchange(src, slots, mine, peers, send, recv):
        slots[mine] = src[...]
        copies = [
            pltpu.make_async_remote_copy(
                src_ref=src,
                dst_ref=slots.at[mine],
                send_sem=send.at[k],
                recv_sem=recv.at[k],
                device_id=peer,
                device_id_type=pl.DeviceIdType.MESH,
            )
            for k, peer in enumerate(peers)
        ]
        for copy in copies:
            copy.start()
        for copy in copies:
            copy.wait()
        total = slots[0]
        for k in range(1, len(peers) + 1):
            total = total + slots[k]
        return total

    half[...] = exchange(x_ref, by_row, my_row, row_peers, row_send, row_recv)
    out_ref[...] = exchange(half, by_blk, my_blk, blk_peers, blk_send, blk_recv)


def sum_everywhere(values):
    blocks, rows = lax.axis_size("blk"), lax.axis_size("row")
    padded = jnp.pad(values[None, :], ((0, 7), (0, 128 - values.shape[0])))
    tile = padded.shape
    out = pl.pallas_call(
        functools.partial(sum_kernel, blocks, rows),
        out_shape=jax.ShapeDtypeStruct(tile, F32),
        in_specs=[pl.BlockSpec(memory_space=pltpu.VMEM)],
        out_specs=pl.BlockSpec(memory_space=pltpu.VMEM),
        scratch_shapes=[
            pltpu.VMEM((rows,) + tile, F32),
            pltpu.VMEM((blocks,) + tile, F32),
            pltpu.VMEM(tile, F32),
            pltpu.SemaphoreType.DMA((rows - 1,)),
            pltpu.SemaphoreType.DMA((rows - 1,)),
            pltpu.SemaphoreType.DMA((blocks - 1,)),
            pltpu.SemaphoreType.DMA((blocks - 1,)),
        ],
        compiler_params=pltpu.CompilerParams(collective_id=0, has_side_effects=True),
        name="sum_everywhere",
    )(padded)
    return out[0, : values.shape[0]]


def mask_pairs(mask, blocks, rows, returning):
    pairs = []
    for blk in range(blocks):
        for row in range(rows):
            partner = blk ^ mask
            source_row = row ^ 6 if blk > partner else row
            here, there = blk * rows + row, partner * rows + source_row
            pairs.append((here, there) if returning else (there, here))
    return pairs


def route(payload, mask, returning):
    blocks, rows = lax.axis_size("blk"), lax.axis_size("row")
    branches = [
        functools.partial(
            lambda pairs, v: lax.ppermute(v, ("blk", "row"), pairs),
            mask_pairs(m, blocks, rows, returning),
        )
        for m in range(1, blocks)
    ]
    return lax.switch(mask - 1, branches, payload)


def row_swap(payload, flip):
    rows = lax.axis_size("row")
    return lax.ppermute(payload, "row", [(i, i ^ flip) for i in range(rows)])


def shards(points, feature_scale, directions, accumulated, plan):
    rows, feat = points.shape
    block_size = rows * lax.axis_size("row")
    total_points = block_size * lax.axis_size("blk")
    amplitude = 512.0 / math.sqrt(block_size)
    scaled = (points.astype(F32) * feature_scale[None, :] / math.sqrt(feat)).astype(BF16)
    dirs = directions.astype(BF16)
    packed = dirs.T.reshape(32, rows // feat, feat).transpose(1, 0, 2).reshape(-1, feat)
    payload = jnp.concatenate([scaled, packed], axis=0)
    masks = [plan[k, 0] for k in range(plan.shape[0])]
    beside = row_swap(payload, 1)
    near = [route(payload, m, False) for m in masks]
    far = [row_swap(v, 2) for v in near]
    fwd_near = [tile_pass(payload, beside, v, rows) for v in near]
    fwd_far = [tile_pass(payload, beside, v, rows) for v in far]
    fwd = fwd_near[0][0] + fwd_near[1][0] + fwd_far[0][0] + fwd_far[1][0]
    own, other = fwd[:, :rows], fwd[:, rows:]
    wide = dirs.astype(F32)
    dirs_beside = beside[rows:].reshape(rows // feat, 32, feat).transpose(1, 0, 2).reshape(32, rows)
    summed = (
        own
        + row_swap(other.astype(BF16), 1).astype(F32)
    )
    for k, m in enumerate(masks):
        returned = fwd_near[k][1] + row_swap(fwd_far[k][1].astype(BF16), 2).astype(F32)
        summed = summed + route(returned.astype(BF16), m, True).astype(F32)
    product = accumulated + amplitude * summed.T
    early = jnp.sum(wide * accumulated, axis=0) + (2.0 * amplitude) * (
        jnp.sum(wide.T * own, axis=1) + jnp.sum(dirs_beside.astype(F32) * other, axis=1)
    )
    curvature = sum_everywhere(early)
    return (product, curvature / total_points)


def solution(mesh):
    return jax.shard_map(
        shards,
        mesh=mesh,
        in_specs=(
            P(("blk", "row"), None),
            P(),
            P(("blk", "row"), None),
            P(("blk", "row"), None),
            P(),
        ),
        out_specs=(P(("blk", "row"), None), P()),
        check_vma=False,
    )
```

```python
import functools
import math

import jax
import jax.numpy as jnp
from jax import lax
from jax.experimental import pallas as pl
from jax.experimental.pallas import tpu as pltpu
from jax.sharding import PartitionSpec as P

F32 = jnp.float32
BF16 = jnp.bfloat16
CHUNK = 256
PIECE = 4
MESH = pl.DeviceIdType.MESH


def widen(z, mine):
    n = -0.5 * jnp.sum(jnp.square(z.astype(F32)), axis=1, keepdims=True)
    high = n.astype(BF16).astype(F32)
    mid = (n - high).astype(BF16).astype(F32)
    low = n - high - mid
    lane = lax.broadcasted_iota(jnp.int32, z.shape, 1)
    own, other = (0, 3) if mine else (3, 0)
    one = jnp.where((lane >= other) & (lane < other + 3), 1.0, 0.0)
    pieces = jnp.where(
        lane == own, high, jnp.where(lane == own + 1, mid, jnp.where(lane == own + 2, low, one))
    )
    return pieces.astype(BF16)


def flip_bit(index, bit):
    return index + bit - 2 * bit * ((index // bit) % 2)


def send(src, dst, sems, peer):
    return pltpu.make_async_remote_copy(
        src_ref=src,
        dst_ref=dst,
        send_sem=sems[0],
        recv_sem=sems[1],
        device_id=peer,
        device_id_type=MESH,
    )


def gather_sum(src, slots, mine, peers, sems):
    slots[mine] = src[...]
    copies = [
        send(src, slots.at[mine], (sems.at[0, k], sems.at[1, k]), peer)
        for k, peer in enumerate(peers)
    ]
    for copy in copies:
        copy.start()
    for copy in copies:
        copy.wait()
    total = slots[0]
    for k in range(1, len(peers) + 1):
        total = total + slots[k]
    return total


def pass_kernel(
    axes,
    rows,
    amplitude,
    payload,
    beside,
    near_1,
    near_2,
    early,
    own_out,
    back_1_out,
    back_2_out,
    curvature_out,
    src,
    wide_a,
    wide_b,
    dirs_a,
    k0,
    k1,
    t0,
    t1,
    fwd,
    back,
    sum_send,
    sum_recv,
    part,
    half,
    by_row,
    by_blk,
    far_sems,
    sum_sems,
    row_sems,
    blk_sems,
):
    blocks, along = axes
    feat = payload.shape[1]
    stride = CHUNK + 32 * (CHUNK // feat)
    chunks = rows // CHUNK
    pieces = chunks // PIECE
    my_blk, my_row = lax.axis_index("blk"), lax.axis_index("row")
    row_peers = [(my_blk, lax.rem(my_row + k, along)) for k in range(1, along)]
    blk_peers = [(lax.rem(my_blk + k, blocks), my_row) for k in range(1, blocks)]
    side = (my_blk, flip_bit(my_row, 1))
    across = (my_blk, flip_bit(my_row, 2))
    barrier = pltpu.get_barrier_semaphore()
    for peer in row_peers + blk_peers:
        pl.semaphore_signal(barrier, inc=1, device_id=peer, device_id_type=MESH)
    pl.semaphore_wait(barrier, along + blocks - 2)

    def far_copy(near, k, q):
        at = pl.ds(q * PIECE * stride, PIECE * stride)
        n = k * pieces + q
        return send(near.at[at], src.at[2 + k, at], (far_sems.at[0, n], far_sems.at[1, n]), across)

    far_copies = [
        far_copy(near, k, q) for k, near in enumerate((near_1, near_2)) for q in range(pieces)
    ]
    for copy in far_copies:
        copy.start()
    src[0] = near_1[...]
    src[1] = near_2[...]
    fwd[...] = jnp.zeros_like(fwd)
    back[...] = jnp.zeros_like(back)

    @pl.loop(0, chunks)
    def _(c):
        at = pl.multiple_of(c * stride, 64)
        for n, ref in enumerate((payload, beside)):
            z = ref[pl.ds(at, CHUNK), :]
            to = pl.ds(pl.multiple_of(n * rows + c * CHUNK, CHUNK), CHUNK)
            wide_a[to, :feat] = z
            wide_a[to, feat:] = widen(z, True)
            for g in range(CHUNK // feat):
                dirs_a[:, pl.ds(pl.multiple_of(n * rows + c * CHUNK + g * feat, feat), feat)] = ref[
                    pl.ds(at + CHUNK + 32 * g, 32), :
                ]

    def chunk_at(g):
        phase, c = g // chunks, g % chunks
        return phase, pl.multiple_of(c * stride, 64), pl.multiple_of(c * CHUNK, CHUNK)

    def prepare(g):
        phase, at, _ = chunk_at(g)
        z = src[phase, pl.ds(at, CHUNK), :]
        slot = g % (2 * PIECE)
        wide_b[slot, :, :feat] = z
        wide_b[slot, :, feat:] = widen(z, False)

    kernels = ((k0, t0), (k1, t1))

    def produce(g, n):
        exponent = lax.dot_general(
            wide_a[n * rows : (n + 1) * rows, :],
            wide_b[g % (2 * PIECE)],
            (((1,), (1,)), ((), ())),
            preferred_element_type=F32,
        )
        kernel = jnp.exp(exponent).astype(BF16)
        kernels[n][0][...] = kernel
        kernels[n][1][...] = kernel.T

    def consume(g, n):
        phase, at, j = chunk_at(g)
        dirs_b = jnp.concatenate(
            [src[phase, pl.ds(at + CHUNK + 32 * k, 32), :] for k in range(CHUNK // feat)], axis=1
        )
        mine = slice(n * rows, (n + 1) * rows)
        fwd[:, mine] += jnp.dot(dirs_b, kernels[n][1][...], preferred_element_type=F32)
        back[phase, :, pl.ds(j, CHUNK)] += jnp.dot(
            dirs_a[:, mine], kernels[n][0][...], preferred_element_type=F32
        )

    for u in range(PIECE):
        prepare(u)
    produce(0, 0)
    steps = 4 * pieces

    def back_copy(k):
        return send(
            sum_send.at[k], sum_recv.at[k], (sum_sems.at[0, k], sum_sems.at[1, k]), across
        )

    @pl.loop(0, steps)
    def _(h):
        for n in range(2 * pieces):
            @pl.when(h == 2 * pieces - 1 + n)
            def _():
                far_copies[n].wait_recv()

        @pl.when(h == 3 * pieces)
        def _():
            sum_send[0] = back[2].astype(BF16)
            back_copy(0).start()

        for u in range(PIECE):
            prepare(jnp.minimum(h + 1, steps - 1) * PIECE + u)
        for u in range(PIECE):
            g = h * PIECE + u
            produce(g, 1)
            consume(g, 0)
            produce(jnp.minimum(g + 1, steps * PIECE - 1), 0)
            consume(g, 1)

    sum_send[1] = back[3].astype(BF16)
    back_copy(1).start()
    sum_send[2] = fwd[:, rows:].astype(BF16)
    fwd_copy = send(
        sum_send.at[2], sum_recv.at[2], (sum_sems.at[0, 2], sum_sems.at[1, 2]), side
    )
    fwd_copy.start()
    products = dirs_a[...].astype(F32) * fwd[...]
    total = jnp.sum(products, axis=1, keepdims=True) * (2.0 * amplitude)
    lane = lax.broadcasted_iota(jnp.int32, (32, 128), 1)
    sublane = lax.broadcasted_iota(jnp.int32, (32, 128), 0)
    flat = jnp.sum(jnp.where(lane == sublane, total, 0.0), axis=0, keepdims=True)
    part[...] = early[...] + flat
    half[...] = gather_sum(part, by_row, my_row, row_peers, row_sems)
    curvature_out[...] = gather_sum(half, by_blk, my_blk, blk_peers, blk_sems)
    for copy in far_copies:
        copy.wait_send()
    back_copy(0).wait()
    back_1_out[...] = (back[0] + sum_recv[0].astype(F32)).astype(BF16)
    fwd_copy.wait()
    own_out[...] = fwd[:, :rows] + sum_recv[2].astype(F32)
    back_copy(1).wait()
    back_2_out[...] = (back[1] + sum_recv[1].astype(F32)).astype(BF16)


def pass_all(payload, beside, near_1, near_2, early, rows, amplitude):
    feat = payload.shape[1]
    axes = (lax.axis_size("blk"), lax.axis_size("row"))
    pieces = rows // CHUNK // PIECE
    tile = (8, 128)
    sums = (32, rows)
    return pl.pallas_call(
        functools.partial(pass_kernel, axes, rows, amplitude),
        out_shape=(
            jax.ShapeDtypeStruct(sums, F32),
            jax.ShapeDtypeStruct(sums, BF16),
            jax.ShapeDtypeStruct(sums, BF16),
            jax.ShapeDtypeStruct(tile, F32),
        ),
        in_specs=[pl.BlockSpec(memory_space=pltpu.VMEM)] * 5,
        out_specs=[pl.BlockSpec(memory_space=pltpu.VMEM)] * 4,
        scratch_shapes=[
            pltpu.VMEM((4,) + payload.shape, BF16),
            pltpu.VMEM((2 * rows, 2 * feat), BF16),
            pltpu.VMEM((2 * PIECE, CHUNK, 2 * feat), BF16),
            pltpu.VMEM((32, 2 * rows), BF16),
            pltpu.VMEM((rows, CHUNK), BF16),
            pltpu.VMEM((rows, CHUNK), BF16),
            pltpu.VMEM((CHUNK, rows), BF16),
            pltpu.VMEM((CHUNK, rows), BF16),
            pltpu.VMEM((32, 2 * rows), F32),
            pltpu.VMEM((4,) + sums, F32),
            pltpu.VMEM((3,) + sums, BF16),
            pltpu.VMEM((3,) + sums, BF16),
            pltpu.VMEM(tile, F32),
            pltpu.VMEM(tile, F32),
            pltpu.VMEM((axes[1],) + tile, F32),
            pltpu.VMEM((axes[0],) + tile, F32),
            pltpu.SemaphoreType.DMA((2, 2 * pieces)),
            pltpu.SemaphoreType.DMA((2, 3)),
            pltpu.SemaphoreType.DMA((2, axes[1] - 1)),
            pltpu.SemaphoreType.DMA((2, axes[0] - 1)),
        ],
        compiler_params=pltpu.CompilerParams(
            collective_id=0, has_side_effects=True, vmem_limit_bytes=48 * 2**20
        ),
        cost_estimate=pl.CostEstimate(
            flops=4 * 4 * rows * rows * 640, bytes_accessed=8 * 2**20, transcendentals=0
        ),
        name="pass_all",
    )(payload, beside, near_1, near_2, early)


def mask_pairs(mask, blocks, rows, returning):
    pairs = []
    for blk in range(blocks):
        for row in range(rows):
            partner = blk ^ mask
            source_row = row ^ 6 if blk > partner else row
            here, there = blk * rows + row, partner * rows + source_row
            pairs.append((here, there) if returning else (there, here))
    return pairs


def route(payload, mask, returning):
    blocks, rows = lax.axis_size("blk"), lax.axis_size("row")
    branches = [
        functools.partial(
            lambda pairs, v: lax.ppermute(v, ("blk", "row"), pairs),
            mask_pairs(m, blocks, rows, returning),
        )
        for m in range(1, blocks)
    ]
    return lax.switch(mask - 1, branches, payload)


def row_swap(payload, flip):
    rows = lax.axis_size("row")
    return lax.ppermute(payload, "row", [(i, i ^ flip) for i in range(rows)])


def shards(points, feature_scale, directions, accumulated, plan):
    rows, feat = points.shape
    block_size = rows * lax.axis_size("row")
    total_points = block_size * lax.axis_size("blk")
    amplitude = 512.0 / math.sqrt(block_size)
    scaled = (points.astype(F32) * feature_scale[None, :] / math.sqrt(feat)).astype(BF16)
    dirs = directions.astype(BF16)
    packed = dirs.T.reshape(32, rows // feat, feat).transpose(1, 0, 2).reshape(rows // CHUNK, -1, feat)
    payload = jnp.concatenate([scaled.reshape(-1, CHUNK, feat), packed], axis=1).reshape(-1, feat)
    masks = [plan[k, 0] for k in range(plan.shape[0])]
    beside = row_swap(payload, 1)
    near = [route(payload, m, False) for m in masks]
    early = jnp.sum(dirs.astype(F32) * accumulated, axis=0)
    early = jnp.pad(early[None, :], ((0, 7), (0, 128 - early.shape[0])))
    own, back_1, back_2, curvature = pass_all(
        payload, beside, near[0], near[1], early, rows, amplitude
    )
    summed = own
    for m, returned in zip(masks, (back_1, back_2)):
        summed = summed + route(returned, m, True).astype(F32)
    product = accumulated + amplitude * summed.T
    return (product, curvature[0, : dirs.shape[1]] / total_points)


def solution(mesh):
    return jax.shard_map(
        shards,
        mesh=mesh,
        in_specs=(
            P(("blk", "row"), None),
            P(),
            P(("blk", "row"), None),
            P(("blk", "row"), None),
            P(),
        ),
        out_specs=(P(("blk", "row"), None), P()),
        check_vma=False,
    )
```

```python
import functools
import math

import jax
import jax.numpy as jnp
from jax import lax
from jax.experimental import pallas as pl
from jax.experimental.pallas import tpu as pltpu
from jax.sharding import PartitionSpec as P

F32 = jnp.float32
BF16 = jnp.bfloat16
CHUNK = 256
PIECE = 2
MESH = pl.DeviceIdType.MESH


def widen(z, mine):
    n = -0.5 * jnp.sum(jnp.square(z.astype(F32)), axis=1, keepdims=True)
    high = n.astype(BF16).astype(F32)
    mid = (n - high).astype(BF16).astype(F32)
    low = n - high - mid
    lane = lax.broadcasted_iota(jnp.int32, z.shape, 1)
    own, other = (0, 3) if mine else (3, 0)
    one = jnp.where((lane >= other) & (lane < other + 3), 1.0, 0.0)
    pieces = jnp.where(
        lane == own, high, jnp.where(lane == own + 1, mid, jnp.where(lane == own + 2, low, one))
    )
    return pieces.astype(BF16)


def flip_bit(index, bit):
    return index + bit - 2 * bit * ((index // bit) % 2)


def send(src, dst, sems, peer):
    return pltpu.make_async_remote_copy(
        src_ref=src,
        dst_ref=dst,
        send_sem=sems[0],
        recv_sem=sems[1],
        device_id=peer,
        device_id_type=MESH,
    )


def gather_sum(src, slots, mine, peers, sems):
    slots[mine] = src[...]
    copies = [
        send(src, slots.at[mine], (sems.at[0, k], sems.at[1, k]), peer)
        for k, peer in enumerate(peers)
    ]
    for copy in copies:
        copy.start()
    for copy in copies:
        copy.wait()
    total = slots[0]
    for k in range(1, len(peers) + 1):
        total = total + slots[k]
    return total


def pass_kernel(
    axes,
    rows,
    amplitude,
    payload,
    beside,
    near_1,
    lead,
    bits,
    early,
    own_out,
    back_2_out,
    curvature_out,
    src,
    wide_a,
    wide_b,
    dirs_a,
    k0,
    k1,
    t0,
    t1,
    fwd,
    back,
    sum_send,
    sum_recv,
    part,
    half,
    by_row,
    by_blk,
    arrived,
    after,
    held,
    came,
    hop_sems,
    give_sems,
    far_sems,
    sum_sems,
    row_sems,
    blk_sems,
):
    blocks, along = axes
    feat = payload.shape[1]
    stride = CHUNK + 32 * (CHUNK // feat)
    chunks = rows // CHUNK
    pieces = chunks // PIECE
    my_blk, my_row = lax.axis_index("blk"), lax.axis_index("row")
    row_peers = [(my_blk, lax.rem(my_row + k, along)) for k in range(1, along)]
    blk_peers = [(lax.rem(my_blk + k, blocks), my_row) for k in range(1, blocks)]
    side = (my_blk, flip_bit(my_row, 1))
    across = (my_blk, flip_bit(my_row, 2))
    barrier = pltpu.get_barrier_semaphore()
    for peer in row_peers + blk_peers:
        pl.semaphore_signal(barrier, inc=1, device_id=peer, device_id_type=MESH)
    pl.semaphore_wait(barrier, along + blocks - 2)

    def piece_at(q):
        return pl.ds(pl.multiple_of(q * PIECE * stride, PIECE * stride), PIECE * stride)

    def hop_copy(n, q):
        at = piece_at(q)
        own = lead if n == 0 else after.at[n - 1]
        y_near, y_far = flip_bit(my_blk, 2), flip_bit(flip_bit(my_blk, 2), 4)
        peer = (
            (y_near, my_row),
            (y_far, my_row),
            (flip_bit(my_blk, 8), my_row),
            (my_blk, flip_bit(flip_bit(my_row, 2), 4)),
        )[n]
        return send(
            own.at[at], arrived.at[n, at], (hop_sems.at[0, n, q], hop_sems.at[1, n, q]), peer
        )

    def take_hop(n, q):
        at = piece_at(q)
        hop_copy(n, q).wait_recv()
        own = lead[at, :] if n == 0 else after[n - 1, at, :]
        taken = jnp.where(bits[n] == 1, arrived[n, at, :], own)
        if n < 3:
            after[n, at, :] = taken
            hop_copy(n + 1, q).start()
        else:
            src[1, at, :] = taken
            far_copy(1, q).start()

    def give_copy(n):
        y_near, y_far = flip_bit(my_blk, 2), flip_bit(flip_bit(my_blk, 2), 4)
        peer = (
            (my_blk, flip_bit(flip_bit(my_row, 2), 4)),
            (flip_bit(my_blk, 1), my_row),
            (flip_bit(my_blk, 8), my_row),
            (y_near, my_row),
            (y_far, my_row),
        )[n]
        return send(held.at[n], came.at[n], (give_sems.at[0, n], give_sems.at[1, n]), peer)

    def take_give(n):
        give_copy(n).wait_recv()
        held[n + 1] = jnp.where(bits[4 + n] == 1, came[n], held[n])
        if n < 4:
            give_copy(n + 1).start()

    def far_copy(k, q):
        at = piece_at(q)
        near = near_1 if k == 0 else src.at[1]
        return send(
            near.at[at], src.at[2 + k, at], (far_sems.at[0, k, q], far_sems.at[1, k, q]), across
        )

    for q in range(pieces):
        hop_copy(0, q).start()
        far_copy(0, q).start()
    src[0] = near_1[...]
    fwd[...] = jnp.zeros_like(fwd)
    back[...] = jnp.zeros_like(back)

    @pl.loop(0, chunks)
    def _(c):
        at = pl.multiple_of(c * stride, 64)
        for n, ref in enumerate((payload, beside)):
            z = ref[pl.ds(at, CHUNK), :]
            to = pl.ds(pl.multiple_of(n * rows + c * CHUNK, CHUNK), CHUNK)
            wide_a[to, :feat] = z
            wide_a[to, feat:] = widen(z, True)
            for g in range(CHUNK // feat):
                dirs_a[:, pl.ds(pl.multiple_of(n * rows + c * CHUNK + g * feat, feat), feat)] = ref[
                    pl.ds(at + CHUNK + 32 * g, 32), :
                ]

    def chunk_at(g):
        h, u = g // PIECE, g % PIECE
        second, k = h // (2 * pieces), h % (2 * pieces)
        late = ((k + 1) % 2) * (1 - (8 - k) // 8) + k // 7
        far = (1 - second) * (k // pieces) + second * late
        piece = (1 - second) * (k % pieces) + second * ((k + 1 - 2 * late) // 2)
        phase, c = second + 2 * far, piece * PIECE + u
        return phase, pl.multiple_of(c * stride, 64), pl.multiple_of(c * CHUNK, CHUNK)

    def prepare(g):
        phase, at, _ = chunk_at(g)
        z = src[phase, pl.ds(at, CHUNK), :]
        slot = g % (2 * PIECE)
        wide_b[slot, :, :feat] = z
        wide_b[slot, :, feat:] = widen(z, False)

    kernels = ((k0, t0), (k1, t1))

    def produce(g, n):
        exponent = lax.dot_general(
            wide_a[n * rows : (n + 1) * rows, :],
            wide_b[g % (2 * PIECE)],
            (((1,), (1,)), ((), ())),
            preferred_element_type=F32,
        )
        kernel = jnp.exp(exponent).astype(BF16)
        kernels[n][0][...] = kernel
        kernels[n][1][...] = kernel.T

    def consume(g, n):
        phase, at, j = chunk_at(g)
        dirs_b = jnp.concatenate(
            [src[phase, pl.ds(at + CHUNK + 32 * k, 32), :] for k in range(CHUNK // feat)], axis=1
        )
        mine = slice(n * rows, (n + 1) * rows)
        fwd[:, mine] += jnp.dot(dirs_b, kernels[n][1][...], preferred_element_type=F32)
        back[phase, :, pl.ds(j, CHUNK)] += jnp.dot(
            dirs_a[:, mine], kernels[n][0][...], preferred_element_type=F32
        )

    for u in range(PIECE):
        prepare(u)
    produce(0, 0)
    steps = 4 * pieces

    def back_copy(k):
        return send(
            sum_send.at[k], sum_recv.at[k], (sum_sems.at[0, k], sum_sems.at[1, k]), across
        )

    @pl.loop(0, steps)
    def _(h):
        @pl.when((h >= pieces - 1) & (h < 2 * pieces - 1))
        def _():
            far_copy(0, h - (pieces - 1)).wait_recv()

        for n in range(4):
            @pl.when((h >= 2 * n + 1) & (h < 2 * n + 6) & (h != 2 * n + 3))
            def _():
                take_hop(n, (2 * (h - (2 * n + 1)) + 1) // 3)

        @pl.when((h % 2 == 1) & (h >= 9) & (h < 7 + 2 * pieces))
        def _():
            far_copy(1, h // 2 - 4).wait_recv()

        @pl.when(h == 6 + 2 * pieces)
        def _():
            far_copy(1, pieces - 1).wait_recv()

        @pl.when(h == 2 * pieces)
        def _():
            sum_send[0] = back[2].astype(BF16)
            back_copy(0).start()

        @pl.when(h == 2 * pieces + 2)
        def _():
            back_copy(0).wait_recv()
            held[0] = (back[0] + sum_recv[0].astype(F32)).astype(BF16)
            give_copy(0).start()

        for n, when in enumerate((4, 5, 7)):
            @pl.when(h == 2 * pieces + when)
            def _():
                take_give(n)

        for u in range(PIECE):
            prepare(jnp.minimum(h + 1, steps - 1) * PIECE + u)
        for u in range(PIECE):
            g = h * PIECE + u
            produce(g, 1)
            consume(g, 0)
            produce(jnp.minimum(g + 1, steps * PIECE - 1), 0)
            consume(g, 1)

    sum_send[1] = back[3].astype(BF16)
    back_copy(1).start()
    sum_send[2] = fwd[:, rows:].astype(BF16)
    fwd_copy = send(
        sum_send.at[2], sum_recv.at[2], (sum_sems.at[0, 2], sum_sems.at[1, 2]), side
    )
    fwd_copy.start()
    products = dirs_a[...].astype(F32) * fwd[...]
    total = jnp.sum(products, axis=1, keepdims=True) * (2.0 * amplitude)
    lane = lax.broadcasted_iota(jnp.int32, (32, 128), 1)
    sublane = lax.broadcasted_iota(jnp.int32, (32, 128), 0)
    flat = jnp.sum(jnp.where(lane == sublane, total, 0.0), axis=0, keepdims=True)
    part[...] = early[...] + flat
    take_give(3)
    half[...] = gather_sum(part, by_row, my_row, row_peers, row_sems)
    curvature_out[...] = gather_sum(half, by_blk, my_blk, blk_peers, blk_sems)
    for q in range(pieces):
        far_copy(0, q).wait_send()
        far_copy(1, q).wait_send()
        for n in range(4):
            hop_copy(n, q).wait_send()
    take_give(4)
    back_copy(0).wait_send()
    for n in range(5):
        give_copy(n).wait_send()
    fwd_copy.wait()
    own_out[...] = fwd[:, :rows] + sum_recv[2].astype(F32) + held[5].astype(F32)
    back_copy(1).wait()
    back_2_out[...] = (back[1] + sum_recv[1].astype(F32)).astype(BF16)


def pass_all(payload, beside, near_1, lead, bits, early, rows, amplitude):
    feat = payload.shape[1]
    axes = (lax.axis_size("blk"), lax.axis_size("row"))
    pieces = rows // CHUNK // PIECE
    tile = (8, 128)
    sums = (32, rows)
    return pl.pallas_call(
        functools.partial(pass_kernel, axes, rows, amplitude),
        out_shape=(
            jax.ShapeDtypeStruct(sums, F32),
            jax.ShapeDtypeStruct(sums, BF16),
            jax.ShapeDtypeStruct(tile, F32),
        ),
        in_specs=[pl.BlockSpec(memory_space=pltpu.VMEM)] * 4
        + [pl.BlockSpec(memory_space=pltpu.SMEM), pl.BlockSpec(memory_space=pltpu.VMEM)],
        out_specs=[pl.BlockSpec(memory_space=pltpu.VMEM)] * 3,
        scratch_shapes=[
            pltpu.VMEM((4,) + payload.shape, BF16),
            pltpu.VMEM((2 * rows, 2 * feat), BF16),
            pltpu.VMEM((2 * PIECE, CHUNK, 2 * feat), BF16),
            pltpu.VMEM((32, 2 * rows), BF16),
            pltpu.VMEM((rows, CHUNK), BF16),
            pltpu.VMEM((rows, CHUNK), BF16),
            pltpu.VMEM((CHUNK, rows), BF16),
            pltpu.VMEM((CHUNK, rows), BF16),
            pltpu.VMEM((32, 2 * rows), F32),
            pltpu.VMEM((4,) + sums, F32),
            pltpu.VMEM((3,) + sums, BF16),
            pltpu.VMEM((3,) + sums, BF16),
            pltpu.VMEM(tile, F32),
            pltpu.VMEM(tile, F32),
            pltpu.VMEM((axes[1],) + tile, F32),
            pltpu.VMEM((axes[0],) + tile, F32),
            pltpu.VMEM((4,) + payload.shape, BF16),
            pltpu.VMEM((3,) + payload.shape, BF16),
            pltpu.VMEM((6,) + sums, BF16),
            pltpu.VMEM((5,) + sums, BF16),
            pltpu.SemaphoreType.DMA((2, 4, pieces)),
            pltpu.SemaphoreType.DMA((2, 5)),
            pltpu.SemaphoreType.DMA((2, 2, pieces)),
            pltpu.SemaphoreType.DMA((2, 3)),
            pltpu.SemaphoreType.DMA((2, axes[1] - 1)),
            pltpu.SemaphoreType.DMA((2, axes[0] - 1)),
        ],
        compiler_params=pltpu.CompilerParams(
            collective_id=0, has_side_effects=True, vmem_limit_bytes=48 * 2**20
        ),
        cost_estimate=pl.CostEstimate(
            flops=4 * 4 * rows * rows * 640, bytes_accessed=8 * 2**20, transcendentals=0
        ),
        name="pass_all",
    )(payload, beside, near_1, lead, bits, early)


def mask_pairs(mask, blocks, rows, returning):
    pairs = []
    for blk in range(blocks):
        for row in range(rows):
            partner = blk ^ mask
            source_row = row ^ 6 if blk > partner else row
            here, there = blk * rows + row, partner * rows + source_row
            pairs.append((here, there) if returning else (there, here))
    return pairs


def route(payload, mask, returning):
    blocks, rows = lax.axis_size("blk"), lax.axis_size("row")
    branches = [
        functools.partial(
            lambda pairs, v: lax.ppermute(v, ("blk", "row"), pairs),
            mask_pairs(m, blocks, rows, returning),
        )
        for m in range(1, blocks)
    ]
    return lax.switch(mask - 1, branches, payload)


def row_swap(payload, flip):
    rows = lax.axis_size("row")
    return lax.ppermute(payload, "row", [(i, i ^ flip) for i in range(rows)])


def shards(points, feature_scale, directions, accumulated, plan):
    rows, feat = points.shape
    block_size = rows * lax.axis_size("row")
    total_points = block_size * lax.axis_size("blk")
    amplitude = 512.0 / math.sqrt(block_size)
    scaled = (points.astype(F32) * feature_scale[None, :] / math.sqrt(feat)).astype(BF16)
    dirs = directions.astype(BF16)
    packed = dirs.T.reshape(32, rows // feat, feat).transpose(1, 0, 2).reshape(rows // CHUNK, -1, feat)
    payload = jnp.concatenate([scaled.reshape(-1, CHUNK, feat), packed], axis=1).reshape(-1, feat)
    masks = [plan[k, 0] for k in range(plan.shape[0])]
    beside = row_swap(payload, 1)
    blocks = lax.axis_size("blk")
    core = lax.ppermute(payload, "blk", [(i, i ^ 1) for i in range(blocks)])
    near_1 = route(payload, masks[0], False)
    near_1, core = lax.optimization_barrier((near_1, core))
    lead = jnp.where(masks[1] % 2 == 1, core, payload)
    my_blk = lax.axis_index("blk")
    flip_1, flip_2 = [
        (jnp.bitwise_xor(my_blk, m) < my_blk).astype(jnp.int32) for m in masks
    ]
    y_1, y_2 = [m // 2 % 4 for m in masks]
    bits = jnp.stack(
        [(y_2 + 1) // 2 % 2, y_2 // 2, masks[1] // 8, flip_2]
        + [flip_1, masks[0] % 2, masks[0] // 8, (y_1 + 1) // 2 % 2, y_1 // 2]
    )
    early = jnp.sum(dirs.astype(F32) * accumulated, axis=0)
    early = jnp.pad(early[None, :], ((0, 7), (0, 128 - early.shape[0])))
    own, back_2, curvature = pass_all(
        payload, beside, near_1, lead, bits, early, rows, amplitude
    )
    summed = own + route(back_2, masks[1], True).astype(F32)
    product = accumulated + amplitude * summed.T
    return (product, curvature[0, : dirs.shape[1]] / total_points)


def solution(mesh):
    return jax.shard_map(
        shards,
        mesh=mesh,
        in_specs=(
            P(("blk", "row"), None),
            P(),
            P(("blk", "row"), None),
            P(("blk", "row"), None),
            P(),
        ),
        out_specs=(P(("blk", "row"), None), P()),
        check_vma=False,
    )
```

```python
import functools
import math

import jax
import jax.numpy as jnp
from jax import lax
from jax.experimental import pallas as pl
from jax.experimental.pallas import tpu as pltpu
from jax.sharding import PartitionSpec as P

F32 = jnp.float32
BF16 = jnp.bfloat16
CHUNK = 256
PIECE = 2
MESH = pl.DeviceIdType.MESH


def widen(z, mine):
    n = -0.5 * jnp.sum(jnp.square(z.astype(F32)), axis=1, keepdims=True)
    high = n.astype(BF16).astype(F32)
    mid = (n - high).astype(BF16).astype(F32)
    low = n - high - mid
    lane = lax.broadcasted_iota(jnp.int32, z.shape, 1)
    own, other = (0, 3) if mine else (3, 0)
    one = jnp.where((lane >= other) & (lane < other + 3), 1.0, 0.0)
    pieces = jnp.where(
        lane == own, high, jnp.where(lane == own + 1, mid, jnp.where(lane == own + 2, low, one))
    )
    return pieces.astype(BF16)


def flip_bit(index, bit):
    return index + bit - 2 * bit * ((index // bit) % 2)


def send(src, dst, sems, peer):
    return pltpu.make_async_remote_copy(
        src_ref=src,
        dst_ref=dst,
        send_sem=sems[0],
        recv_sem=sems[1],
        device_id=peer,
        device_id_type=MESH,
    )


def gather_sum(src, slots, mine, peers, sems):
    slots[mine] = src[...]
    copies = [
        send(src, slots.at[mine], (sems.at[0, k], sems.at[1, k]), peer)
        for k, peer in enumerate(peers)
    ]
    for copy in copies:
        copy.start()
    for copy in copies:
        copy.wait()
    total = slots[0]
    for k in range(1, len(peers) + 1):
        total = total + slots[k]
    return total


def pass_kernel(
    axes,
    rows,
    amplitude,
    payload,
    beside,
    near_1,
    lead,
    bits,
    early,
    own_out,
    back_2_out,
    curvature_out,
    src,
    wide_a,
    wide_b,
    dirs_a,
    k0,
    k1,
    t0,
    t1,
    fwd,
    back,
    sum_send,
    sum_recv,
    part,
    half,
    by_row,
    by_blk,
    arrived,
    after,
    held,
    came,
    hop_sems,
    give_sems,
    far_sems,
    sum_sems,
    row_sems,
    blk_sems,
):
    blocks, along = axes
    feat = payload.shape[1]
    stride = CHUNK + 32 * (CHUNK // feat)
    chunks = rows // CHUNK
    pieces = chunks // PIECE
    my_blk, my_row = lax.axis_index("blk"), lax.axis_index("row")
    row_peers = [(my_blk, lax.rem(my_row + k, along)) for k in range(1, along)]
    blk_peers = [(lax.rem(my_blk + k, blocks), my_row) for k in range(1, blocks)]
    side = (my_blk, flip_bit(my_row, 1))
    across = (my_blk, flip_bit(my_row, 2))
    barrier = pltpu.get_barrier_semaphore()
    for peer in row_peers + blk_peers:
        pl.semaphore_signal(barrier, inc=1, device_id=peer, device_id_type=MESH)

    def piece_at(q):
        return pl.ds(pl.multiple_of(q * PIECE * stride, PIECE * stride), PIECE * stride)

    def hop_copy(n, q):
        at = piece_at(q)
        own = lead if n == 0 else after.at[n - 1]
        y_near, y_far = flip_bit(my_blk, 2), flip_bit(flip_bit(my_blk, 2), 4)
        peer = (
            (y_near, my_row),
            (y_far, my_row),
            (flip_bit(my_blk, 8), my_row),
            (my_blk, flip_bit(flip_bit(my_row, 2), 4)),
        )[n]
        return send(
            own.at[at], arrived.at[n, at], (hop_sems.at[0, n, q], hop_sems.at[1, n, q]), peer
        )

    def take_hop(n, q):
        at = piece_at(q)
        hop_copy(n, q).wait_recv()
        own = lead[at, :] if n == 0 else after[n - 1, at, :]
        taken = jnp.where(bits[n] == 1, arrived[n, at, :], own)
        if n < 3:
            after[n, at, :] = taken
            hop_copy(n + 1, q).start()
        else:
            src[1, at, :] = taken
            far_copy(1, q).start()

    def give_copy(n):
        y_near, y_far = flip_bit(my_blk, 2), flip_bit(flip_bit(my_blk, 2), 4)
        peer = (
            (my_blk, flip_bit(flip_bit(my_row, 2), 4)),
            (flip_bit(my_blk, 1), my_row),
            (flip_bit(my_blk, 8), my_row),
            (y_near, my_row),
            (y_far, my_row),
        )[n]
        return send(held.at[n], came.at[n], (give_sems.at[0, n], give_sems.at[1, n]), peer)

    def take_give(n):
        give_copy(n).wait_recv()
        held[n + 1] = jnp.where(bits[4 + n] == 1, came[n], held[n])
        if n < 4:
            give_copy(n + 1).start()

    def far_copy(k, q):
        at = piece_at(q)
        near = near_1 if k == 0 else src.at[1]
        return send(
            near.at[at], src.at[2 + k, at], (far_sems.at[0, k, q], far_sems.at[1, k, q]), across
        )

    src[0] = near_1[...]
    fwd[...] = jnp.zeros_like(fwd)
    back[...] = jnp.zeros_like(back)

    @pl.loop(0, chunks)
    def _(c):
        at = pl.multiple_of(c * stride, 64)
        for n, ref in enumerate((payload, beside)):
            z = ref[pl.ds(at, CHUNK), :]
            to = pl.ds(pl.multiple_of(n * rows + c * CHUNK, CHUNK), CHUNK)
            wide_a[to, :feat] = z
            wide_a[to, feat:] = widen(z, True)
            for g in range(CHUNK // feat):
                dirs_a[:, pl.ds(pl.multiple_of(n * rows + c * CHUNK + g * feat, feat), feat)] = ref[
                    pl.ds(at + CHUNK + 32 * g, 32), :
                ]

    pl.semaphore_wait(barrier, along + blocks - 2)
    for q in range(pieces):
        hop_copy(0, q).start()
        far_copy(0, q).start()

    def chunk_at(g):
        h, u = g // PIECE, g % PIECE
        second, k = h // (2 * pieces), h % (2 * pieces)
        late = ((k + 1) % 2) * (1 - (8 - k) // 8) + k // 7
        far = (1 - second) * (k // pieces) + second * late
        piece = (1 - second) * (k % pieces) + second * ((k + 1 - 2 * late) // 2)
        phase, c = second + 2 * far, piece * PIECE + u
        return phase, pl.multiple_of(c * stride, 64), pl.multiple_of(c * CHUNK, CHUNK)

    def prepare(g):
        phase, at, _ = chunk_at(g)
        z = src[phase, pl.ds(at, CHUNK), :]
        slot = g % (2 * PIECE)
        wide_b[slot, :, :feat] = z
        wide_b[slot, :, feat:] = widen(z, False)

    kernels = ((k0, t0), (k1, t1))

    def produce(g, n):
        exponent = lax.dot_general(
            wide_a[n * rows : (n + 1) * rows, :],
            wide_b[g % (2 * PIECE)],
            (((1,), (1,)), ((), ())),
            preferred_element_type=F32,
        )
        kernel = jnp.exp(exponent).astype(BF16)
        kernels[n][0][...] = kernel
        kernels[n][1][...] = kernel.T

    def consume(g, n):
        phase, at, j = chunk_at(g)
        dirs_b = jnp.concatenate(
            [src[phase, pl.ds(at + CHUNK + 32 * k, 32), :] for k in range(CHUNK // feat)], axis=1
        )
        mine = slice(n * rows, (n + 1) * rows)
        fwd[:, mine] += jnp.dot(dirs_b, kernels[n][1][...], preferred_element_type=F32)
        back[phase, :, pl.ds(j, CHUNK)] += jnp.dot(
            dirs_a[:, mine], kernels[n][0][...], preferred_element_type=F32
        )

    for u in range(PIECE):
        prepare(u)
    produce(0, 0)
    steps = 4 * pieces

    def back_copy(k):
        return send(
            sum_send.at[k], sum_recv.at[k], (sum_sems.at[0, k], sum_sems.at[1, k]), across
        )

    @pl.loop(0, steps)
    def _(h):
        @pl.when((h >= pieces - 1) & (h < 2 * pieces - 1))
        def _():
            far_copy(0, h - (pieces - 1)).wait_recv()

        for n in range(4):
            @pl.when((h >= 2 * n + 1) & (h < 2 * n + 6) & (h != 2 * n + 3))
            def _():
                take_hop(n, (2 * (h - (2 * n + 1)) + 1) // 3)

        @pl.when((h % 2 == 1) & (h >= 9) & (h < 7 + 2 * pieces))
        def _():
            far_copy(1, h // 2 - 4).wait_recv()

        @pl.when(h == 6 + 2 * pieces)
        def _():
            far_copy(1, pieces - 1).wait_recv()

        @pl.when(h == 2 * pieces)
        def _():
            sum_send[0] = back[2].astype(BF16)
            back_copy(0).start()

        @pl.when(h == 2 * pieces + 2)
        def _():
            back_copy(0).wait_recv()
            held[0] = (back[0] + sum_recv[0].astype(F32)).astype(BF16)
            give_copy(0).start()

        for n, when in enumerate((4, 5, 7)):
            @pl.when(h == 2 * pieces + when)
            def _():
                take_give(n)

        for u in range(PIECE):
            prepare(jnp.minimum(h + 1, steps - 1) * PIECE + u)
        for u in range(PIECE):
            g = h * PIECE + u
            produce(g, 1)
            consume(g, 0)
            produce(jnp.minimum(g + 1, steps * PIECE - 1), 0)
            consume(g, 1)

    sum_send[1] = back[3].astype(BF16)
    back_copy(1).start()
    sum_send[2] = fwd[:, rows:].astype(BF16)
    fwd_copy = send(
        sum_send.at[2], sum_recv.at[2], (sum_sems.at[0, 2], sum_sems.at[1, 2]), side
    )
    fwd_copy.start()
    products = dirs_a[...].astype(F32) * fwd[...]
    total = jnp.sum(products, axis=1, keepdims=True) * (2.0 * amplitude)
    lane = lax.broadcasted_iota(jnp.int32, (32, 128), 1)
    sublane = lax.broadcasted_iota(jnp.int32, (32, 128), 0)
    flat = jnp.sum(jnp.where(lane == sublane, total, 0.0), axis=0, keepdims=True)
    part[...] = early[...] + flat
    take_give(3)
    half[...] = gather_sum(part, by_row, my_row, row_peers, row_sems)
    curvature_out[...] = gather_sum(half, by_blk, my_blk, blk_peers, blk_sems)
    for q in range(pieces):
        far_copy(0, q).wait_send()
        far_copy(1, q).wait_send()
        for n in range(4):
            hop_copy(n, q).wait_send()
    take_give(4)
    back_copy(0).wait_send()
    for n in range(5):
        give_copy(n).wait_send()
    fwd_copy.wait()
    own_out[...] = fwd[:, :rows] + sum_recv[2].astype(F32) + held[5].astype(F32)
    back_copy(1).wait()
    back_2_out[...] = (back[1] + sum_recv[1].astype(F32)).astype(BF16)


def pass_all(payload, beside, near_1, lead, bits, early, rows, amplitude):
    feat = payload.shape[1]
    axes = (lax.axis_size("blk"), lax.axis_size("row"))
    pieces = rows // CHUNK // PIECE
    tile = (8, 128)
    sums = (32, rows)
    return pl.pallas_call(
        functools.partial(pass_kernel, axes, rows, amplitude),
        out_shape=(
            jax.ShapeDtypeStruct(sums, F32),
            jax.ShapeDtypeStruct(sums, BF16),
            jax.ShapeDtypeStruct(tile, F32),
        ),
        in_specs=[pl.BlockSpec(memory_space=pltpu.VMEM)] * 4
        + [pl.BlockSpec(memory_space=pltpu.SMEM), pl.BlockSpec(memory_space=pltpu.VMEM)],
        out_specs=[pl.BlockSpec(memory_space=pltpu.VMEM)] * 3,
        scratch_shapes=[
            pltpu.VMEM((4,) + payload.shape, BF16),
            pltpu.VMEM((2 * rows, 2 * feat), BF16),
            pltpu.VMEM((2 * PIECE, CHUNK, 2 * feat), BF16),
            pltpu.VMEM((32, 2 * rows), BF16),
            pltpu.VMEM((rows, CHUNK), BF16),
            pltpu.VMEM((rows, CHUNK), BF16),
            pltpu.VMEM((CHUNK, rows), BF16),
            pltpu.VMEM((CHUNK, rows), BF16),
            pltpu.VMEM((32, 2 * rows), F32),
            pltpu.VMEM((4,) + sums, F32),
            pltpu.VMEM((3,) + sums, BF16),
            pltpu.VMEM((3,) + sums, BF16),
            pltpu.VMEM(tile, F32),
            pltpu.VMEM(tile, F32),
            pltpu.VMEM((axes[1],) + tile, F32),
            pltpu.VMEM((axes[0],) + tile, F32),
            pltpu.VMEM((4,) + payload.shape, BF16),
            pltpu.VMEM((3,) + payload.shape, BF16),
            pltpu.VMEM((6,) + sums, BF16),
            pltpu.VMEM((5,) + sums, BF16),
            pltpu.SemaphoreType.DMA((2, 4, pieces)),
            pltpu.SemaphoreType.DMA((2, 5)),
            pltpu.SemaphoreType.DMA((2, 2, pieces)),
            pltpu.SemaphoreType.DMA((2, 3)),
            pltpu.SemaphoreType.DMA((2, axes[1] - 1)),
            pltpu.SemaphoreType.DMA((2, axes[0] - 1)),
        ],
        compiler_params=pltpu.CompilerParams(
            collective_id=0, has_side_effects=True, vmem_limit_bytes=48 * 2**20
        ),
        cost_estimate=pl.CostEstimate(
            flops=4 * 4 * rows * rows * 640, bytes_accessed=8 * 2**20, transcendentals=0
        ),
        name="pass_all",
    )(payload, beside, near_1, lead, bits, early)


def mask_pairs(mask, blocks, rows, returning):
    pairs = []
    for blk in range(blocks):
        for row in range(rows):
            partner = blk ^ mask
            source_row = row ^ 6 if blk > partner else row
            here, there = blk * rows + row, partner * rows + source_row
            pairs.append((here, there) if returning else (there, here))
    return pairs


def route(payload, mask, returning):
    blocks, rows = lax.axis_size("blk"), lax.axis_size("row")
    branches = [
        functools.partial(
            lambda pairs, v: lax.ppermute(v, ("blk", "row"), pairs),
            mask_pairs(m, blocks, rows, returning),
        )
        for m in range(1, blocks)
    ]
    return lax.switch(mask - 1, branches, payload)


def row_swap(payload, flip):
    rows = lax.axis_size("row")
    return lax.ppermute(payload, "row", [(i, i ^ flip) for i in range(rows)])


def shards(points, feature_scale, directions, accumulated, plan):
    rows, feat = points.shape
    block_size = rows * lax.axis_size("row")
    total_points = block_size * lax.axis_size("blk")
    amplitude = 512.0 / math.sqrt(block_size)
    scaled = (points.astype(F32) * feature_scale[None, :] / math.sqrt(feat)).astype(BF16)
    dirs = directions.astype(BF16)
    packed = dirs.T.reshape(32, rows // feat, feat).transpose(1, 0, 2).reshape(rows // CHUNK, -1, feat)
    payload = jnp.concatenate([scaled.reshape(-1, CHUNK, feat), packed], axis=1).reshape(-1, feat)
    masks = [plan[k, 0] for k in range(plan.shape[0])]
    beside = row_swap(payload, 1)
    blocks = lax.axis_size("blk")
    core = lax.ppermute(payload, "blk", [(i, i ^ 1) for i in range(blocks)])
    near_1 = route(payload, masks[0], False)
    near_1, core = lax.optimization_barrier((near_1, core))
    lead = jnp.where(masks[1] % 2 == 1, core, payload)
    my_blk = lax.axis_index("blk")
    flip_1, flip_2 = [
        (jnp.bitwise_xor(my_blk, m) < my_blk).astype(jnp.int32) for m in masks
    ]
    y_1, y_2 = [m // 2 % 4 for m in masks]
    bits = jnp.stack(
        [(y_2 + 1) // 2 % 2, y_2 // 2, masks[1] // 8, flip_2]
        + [flip_1, masks[0] % 2, masks[0] // 8, (y_1 + 1) // 2 % 2, y_1 // 2]
    )
    early = jnp.sum(dirs.astype(F32) * accumulated, axis=0)
    early = jnp.pad(early[None, :], ((0, 7), (0, 128 - early.shape[0])))
    own, back_2, curvature = pass_all(
        payload, beside, near_1, lead, bits, early, rows, amplitude
    )
    summed = own + route(back_2, masks[1], True).astype(F32)
    product = accumulated + amplitude * summed.T
    return (product, curvature[0, : dirs.shape[1]] / total_points)


def solution(mesh):
    return jax.shard_map(
        shards,
        mesh=mesh,
        in_specs=(
            P(("blk", "row"), None),
            P(),
            P(("blk", "row"), None),
            P(("blk", "row"), None),
            P(),
        ),
        out_specs=(P(("blk", "row"), None), P()),
        check_vma=False,
    )
```
